512 devices in a mesh: freq: 4 (over z_hi), mom: 128 (over y, z_lo, x, core).
Axes of the slice: x: 4, y: 4, z: 16 (z_hi: 4, z_lo: 4; z = z_hi * 4 + z_lo), core: 2. Of those that a mesh axis runs over, the one named last changes fastest.
Arguments:
- vertex: bfloat16 [4, 512, 512, 512], P('freq', 'mom'), may hold values from -6 to 6
- bubble: float32 [4, 512, 512], P('freq', 'mom'), may hold values from 0.0078125 to 0.0625
- mixing: float32 [4, 4], replicated, may hold values from -3 to 3
- lattice_order: int32 [512], replicated, may hold values from 0 to 511, each once
Outputs:
- converted: bfloat16 [4, 512, 256, 512], P('freq', 'mom')
The draws below stay inside these ranges and needn't reach their ends.
Inputs may be any that keep to these rules, and one draw needn't show every extreme that they name: `lattice_order`: each of the 512 lattice points stands at exactly one index.
All inputs are finite; a program needn't handle non-finite values.
Results may differ from the reference program's by a relative error of at most 0.018.
Values may be sent and summed in bfloat16 or wider, within the bound.
A program may use at most 64 MiB of HBM per device.

```python
import math
import jax
import jax.numpy as jnp
from jax import lax

LX = 32
LY = 16
W = 4
K = 512
KW = 256


def block_levels(key, shape, split, low, high):
    def one(position, shards_of):
        heights = jax.random.uniform(jax.random.fold_in(jax.random.fold_in(key, 6), position), (shards_of,), jnp.float32, low / len(split), high / len(split))
        return jnp.repeat(jnp.exp(heights), shape[position] // shards_of).reshape((-1,) + (1,) * (len(shape) - position - 1))

    level = one(*split[0])
    for cut in split[1:]:
        level = level * one(*cut)
    return level


def bell_draw(own_key, extent, spread, bound, pieces=(), held_as=jnp.bfloat16):
    entries = jax.random.normal(own_key, extent, jnp.float32) * spread
    if len(pieces) > 0:
        entries = block_levels(own_key, extent, pieces, -0.22, 0.18) * entries
    return jnp.clip(entries, min=-bound, max=bound).astype(held_as)


def setup_inputs(seed: int = 0) -> dict:
    splits = jax.random.split(jax.random.key(seed), 5)
    vertex = bell_draw(splits[0], (W, K, K, K), 1.0, 6.0, ((0, 4), (1, 128)))
    bubble = jnp.clip(jnp.exp(math.log(0.0625) - 2.0794415 * jax.random.uniform(splits[1], (W, K, K), jnp.float32) ** block_levels(splits[1], (W, K, K), ((0, 4), (1, 128)), -0.2, 0.2)), 0.0078125, 0.0625)
    mixing = bell_draw(splits[2], (W, W), 0.5, 3.0, (), jnp.float32)
    lattice_order = jax.random.permutation(splits[3], K).astype(jnp.int32)
    return dict(vertex=vertex, bubble=bubble, mixing=mixing, lattice_order=lattice_order)


def lattice_maps(lattice_order):
    places = jnp.argsort(lattice_order).astype(jnp.int32)
    coord_x = lattice_order // LY
    coord_y = lattice_order % LY
    summed = ((coord_x[:, None] + coord_x[None, :]) % LX) * LY + (coord_y[:, None] + coord_y[None, :]) % LY
    differ = ((coord_x[None, :] - coord_x[:, None]) % LX) * LY + (coord_y[None, :] - coord_y[:, None]) % LY
    return jnp.take(places, summed.astype(jnp.int32)), jnp.take(places, differ.astype(jnp.int32))


def ladder_block(vertex_q, bubble_q):
    wide = vertex_q.astype(jnp.float32)
    scaled = (bubble_q[:, :, None] * wide).astype(jnp.bfloat16)
    ladder = (wide + jnp.einsum("wij,wjk->wik", wide, scaled.astype(jnp.float32), precision=lax.Precision.HIGHEST)).astype(jnp.bfloat16)
    scaled = (bubble_q[:, :, None] * ladder.astype(jnp.float32)).astype(jnp.bfloat16)
    return jnp.einsum("wij,wjk->wik", wide[:, :KW, :], scaled.astype(jnp.float32), precision=lax.Precision.HIGHEST).astype(jnp.bfloat16)


def reference(vertex, bubble, mixing, lattice_order):
    add_map, diff_map = lattice_maps(lattice_order)
    reducible = lax.map(lambda pair: ladder_block(pair[0], pair[1]), (jnp.moveaxis(vertex, 1, 0), jnp.moveaxis(bubble, 1, 0)))
    momenta = jnp.arange(K, dtype=jnp.int32)
    window = jnp.arange(KW, dtype=jnp.int32)
    freqs = jnp.arange(W, dtype=jnp.int32)

    def convert(column):
        shifted = add_map[:KW, column]
        crossed = reducible[diff_map[None, :KW, :], freqs[:, None, None], window[None, :, None], shifted[None, :, None]]
        return jnp.einsum("ab,bkl->akl", mixing, crossed.astype(jnp.float32), precision=lax.Precision.HIGHEST).astype(jnp.bfloat16)

    result = lax.map(convert, momenta)
    return jnp.moveaxis(result, 0, 1)
```

```python
import jax
import jax.numpy as jnp
from jax import lax
from jax.experimental import pallas as pl
from jax.experimental.pallas import tpu as pltpu
from jax.sharding import PartitionSpec as P

LX = 32
LY = 16
MESH = pl.DeviceIdType.MESH
F32 = jnp.float32
BF16 = jnp.bfloat16


def dot(a, b, dims=((1,), (0,))):
    return lax.dot_general(a, b, (dims, ((), ())), preferred_element_type=F32)


def iota(shape, axis):
    return lax.broadcasted_iota(jnp.int32, shape, axis)


def one_hot(hit):
    return jnp.where(hit, 1.0, 0.0).astype(BF16)


def zlo_last(r):
    y, xc, zlo, local = r // 128, (r // 16) % 8, (r // 4) % 4, r % 4
    return y * 128 + zlo * 32 + xc * 4 + local


def zlo_second(r):
    y, zlo, xc, local = r // 128, (r // 32) % 4, (r // 4) % 8, r % 4
    return y * 128 + xc * 16 + zlo * 4 + local


def shift_rows(x, kx, ky, sign):
    n = x.shape[-1]
    x = x.reshape(LX, LY, n)
    for bit in range(4):
        rolled = pltpu.roll(x, (-sign * (1 << bit)) % LY, 1)
        x = jnp.where((ky & (1 << bit)) != 0, rolled, x)
    for bit in range(5):
        s = (sign * (1 << bit)) % LX
        rolled = jnp.concatenate([x[s:], x[:s]], axis=0)
        x = jnp.where((kx & (1 << bit)) != 0, rolled, x)
    return x.reshape(LX * LY, n)


def body(v_ref, bub_ref, ord_ref, mix_ref, out_ref,
         tt, ta, tb, tq, pr, pt, da, db, vb, lad, red,
         xa, r1a, ma, r2a, xs, r3, xb, r0, x1, r1b, mb, r2b, dd,
         s1a_s, s1a_r, s2a_s, s2a_r, s3_s, s3_r, s0_s, s0_r, s1b_s, s1b_r, s2b_s, s2b_r):
    f = lax.axis_index("freq")
    m = lax.axis_index("mom")
    core, x, zlo, y = m % 2, (m // 2) % 4, (m // 8) % 4, m // 32
    z = f * 4 + zlo
    here = (y * 4 + x) * 2 + core
    zlo_mix = (zlo + 2) % 4
    slot2 = f * 4 + zlo_mix

    def at_z(freq, low):
        return {"freq": freq, "mom": m - zlo * 8 + low * 8}

    def at_xy(place):
        return {"freq": f, "mom": ((place // 8) * 4 + zlo) * 8 + place % 8}

    barrier = pltpu.get_barrier_semaphore()

    def greet_z(i, _):
        t = (z + i) % 16
        pl.semaphore_signal(barrier, inc=1, device_id=at_z(t // 4, t % 4), device_id_type=MESH)
        return _

    def greet_xy(i, _):
        pl.semaphore_signal(barrier, inc=1, device_id=at_xy((here + i) % 32), device_id_type=MESH)
        return _

    lax.fori_loop(1, 16, greet_z, 0)
    lax.fori_loop(1, 32, greet_xy, 0)

    order = ord_ref[...]
    kx = order[:, :256] // LY
    ky = order[:, :256] % LY
    tt[...] = one_hot(iota((512, 512), 0) == order)
    for b in range(4):
        column = jnp.transpose(jnp.broadcast_to(order[:, b * 128:(b + 1) * 128], (128, 128)))
        for c in range(4):
            ta[b * 128:(b + 1) * 128, c * 128:(c + 1) * 128] = one_hot(
                column == iota((128, 128), 1) + c * 128)
    pr[...] = one_hot(zlo_last(iota((512, 1), 0)) == iota((1, 512), 1))
    tb[...] = dot(pr[...], ta[...]).astype(BF16)

    def send1(src, dst, ssem, rsem, ql, go):
        for j in range(4):
            cp = pltpu.make_async_remote_copy(
                src.at[ql, j], dst.at[ql, f], ssem.at[ql], rsem.at[ql],
                device_id=at_z(j, zlo_mix), device_id_type=MESH)
            cp.start()

    def compute(ql, carry):
        bub = bub_ref[pl.ds(ql, 1), :]
        vb[...] = (v_ref[ql].astype(F32) * bub).astype(BF16)
        for h in range(2):
            rows = pl.ds(h * 256, 256)
            lad[rows, :] = (v_ref[ql, rows, :].astype(F32) + dot(vb[rows, :], v_ref[ql])).astype(BF16)
        red[...] = dot(vb[:256, :], lad[...]).astype(BF16)
        moved = []
        for h in range(2):
            lanes = slice(h * 128, (h + 1) * 128)
            point = dot(tt[...], red[lanes, :], ((1,), (1,)))
            moved.append(shift_rows(point, kx[:, lanes], ky[:, lanes], 1).astype(BF16))
        xa[ql] = dot(ta[...], moved[0]).astype(BF16).reshape(4, 128, 128)
        xb[:, pl.ds(ql, 1)] = dot(tb[...], moved[1]).astype(BF16).reshape(32, 1, 16, 128)

        @pl.when(ql == 0)
        def _():
            pl.semaphore_wait(barrier, 46)

        send1(xa, r1a, s1a_s, s1a_r, ql, None)
        return carry

    lax.fori_loop(0, 4, compute, 0)

    def spread(src, dst, ssem, rsem):
        pltpu.make_async_copy(src.at[here], dst.at[here], rsem).start()

        def one(i, _):
            to = (here + i) % 32
            pltpu.make_async_remote_copy(
                src.at[to], dst.at[here], ssem, rsem, device_id=at_xy(to), device_id_type=MESH).start()
            return _

        lax.fori_loop(1, 32, one, 0)

    def send2(src, dst, ssem, rsem):
        pltpu.make_async_copy(src.at[f, zlo], dst.at[slot2], rsem).start()

        def one(i, _):
            t = (z + i) % 16
            pltpu.make_async_remote_copy(
                src.at[t // 4, t % 4], dst.at[slot2], ssem, rsem,
                device_id=at_z(t // 4, t % 4), device_id_type=MESH).start()
            return _

        lax.fori_loop(1, 16, one, 0)

    def got(ref, sem):
        pltpu.make_async_copy(ref, ref, sem).wait()

    def mix(src, dst, ssem, rsem, ql):
        got(src.at[ql], rsem.at[ql])
        parts = [src[ql, b].astype(F32) for b in range(4)]
        for a in range(4):
            total = mix_ref[a, 0] * parts[0]
            for b in range(1, 4):
                total = total + mix_ref[a, b] * parts[b]
            dst[ql, a] = total.astype(BF16).reshape(4, 32, 128)

    def mix_a(ql, _):
        mix(r1a, ma, s1a_s, s1a_r, ql)
        send2(ma.at[ql], r2a.at[ql], s2a_s.at[ql], s2a_r.at[ql])
        return _

    def mix_b(ql, _):
        mix(r1b, mb, s1b_s, s1b_r, ql)
        send2(mb.at[ql], r2b.at[ql], s2b_s.at[ql], s2b_r.at[ql])
        return _

    spread(xb, r0, s0_s, s0_r)
    pt[...] = one_hot(zlo_second(iota((512, 1), 0)) == iota((1, 512), 1))
    row, col = iota((512, 1), 0), iota((1, 512), 1)
    db[...] = one_hot((row % 128) * 4 + row // 128 == col)
    da[...] = one_hot(zlo_second((row % 128) * 4 + row // 128) == col)
    tq[...] = dot(tt[...], db[...], ((1,), (1,))).astype(BF16)

    lax.fori_loop(0, 2, mix_a, 0)
    got(r0, s0_r)

    def first_b(ql, _):
        rows = r0[:, pl.ds(ql, 1)].reshape(512, 128)
        x1[ql] = dot(pt[...], rows).astype(BF16).reshape(4, 128, 128)
        send1(x1, r1b, s1b_s, s1b_r, ql, None)
        return _

    lax.fori_loop(0, 4, first_b, 0)
    lax.fori_loop(2, 4, mix_a, 0)

    def third_a(ql, _):
        got(r2a.at[ql], s2a_r.at[ql])
        xs[ql] = dot(pr[...], r2a[ql].reshape(512, 128)).astype(BF16).reshape(32, 16, 128)
        spread(xs.at[ql], r3.at[ql], s3_s.at[ql], s3_r.at[ql])
        return mix_b(ql, _)

    lax.fori_loop(0, 4, third_a, 0)

    def finish(h):
        lanes = slice(h * 128, (h + 1) * 128)

        def one(local, _):
            g = dot(tq[...], dd[h, local].reshape(512, 128))
            moved = jnp.transpose(shift_rows(g, kx[:, lanes], ky[:, lanes], -1)).astype(BF16)
            out_ref[local, lanes, :] = dot(moved, tt[...]).astype(BF16)
            return _

        lax.fori_loop(0, 4, one, 0)

    def last_a(ql, _):
        got(r3.at[ql], s3_r.at[ql])
        rows = dot(da[...], r3[ql].reshape(512, 128)).astype(BF16)
        dd[0, :, pl.ds(ql, 1)] = rows.reshape(4, 1, 128, 128)
        return _

    def last_b(ql, _):
        got(r2b.at[ql], s2b_r.at[ql])
        rows = dot(db[...], r2b[ql].reshape(512, 128)).astype(BF16)
        dd[1, :, pl.ds(ql, 1)] = rows.reshape(4, 1, 128, 128)
        return _

    lax.fori_loop(0, 4, last_a, 0)
    finish(0)
    lax.fori_loop(0, 4, last_b, 0)
    finish(1)

    def drain(ql, _):
        got(xa.at[ql], s1a_s.at[ql])
        got(x1.at[ql], s1b_s.at[ql])
        for s in (s2a_s, s2b_s):
            pltpu.make_async_copy(ma.at[ql, pl.ds(0, 3)], ma.at[ql, pl.ds(0, 3)], s.at[ql]).wait()
            pltpu.make_async_copy(ma.at[ql, 0, pl.ds(0, 3)], ma.at[ql, 0, pl.ds(0, 3)], s.at[ql]).wait()
        got(xs.at[ql, pl.ds(0, 31)], s3_s.at[ql])
        return _

    lax.fori_loop(0, 4, drain, 0)
    got(xb.at[pl.ds(0, 31)], s0_s)


def on_device(vertex, bubble, mixing, lattice_order):
    def vm(*shape):
        return pltpu.VMEM(shape, BF16)

    sem = pltpu.SemaphoreType.DMA
    out = pl.pallas_call(
        body,
        out_shape=jax.ShapeDtypeStruct((4, 256, 512), BF16),
        in_specs=[pl.BlockSpec(memory_space=pltpu.VMEM)] * 3 + [pl.BlockSpec(memory_space=pltpu.SMEM)],
        out_specs=pl.BlockSpec(memory_space=pltpu.VMEM),
        scratch_shapes=[
            vm(512, 512), vm(512, 512), vm(512, 512), vm(512, 512),
            vm(512, 512), vm(512, 512), vm(512, 512), vm(512, 512),
            vm(512, 512), vm(512, 512), vm(256, 512),
            vm(4, 4, 128, 128), vm(4, 4, 128, 128), vm(4, 4, 4, 32, 128), vm(4, 16, 32, 128),
            vm(4, 32, 16, 128), vm(4, 32, 16, 128),
            vm(32, 4, 16, 128), vm(32, 4, 16, 128),
            vm(4, 4, 128, 128), vm(4, 4, 128, 128), vm(4, 4, 4, 32, 128), vm(4, 16, 32, 128),
            vm(2, 4, 4, 128, 128),
            sem((4,)), sem((4,)), sem((4,)), sem((4,)), sem((4,)), sem((4,)),
            sem, sem, sem((4,)), sem((4,)), sem((4,)), sem((4,)),
        ],
        compiler_params=pltpu.CompilerParams(
            collective_id=1, has_side_effects=True, vmem_limit_bytes=40 * 2**20),
        cost_estimate=pl.CostEstimate(flops=4 * 10**9, bytes_accessed=4 * 2**20, transcendentals=0),
    )(vertex[0], bubble[0], lattice_order.reshape(1, 512), mixing)
    return out[None]


def solution(mesh):
    in_specs = (P("freq", "mom", None, None), P("freq", "mom", None), P(), P())
    out_specs = P("freq", "mom", None, None)
    return jax.shard_map(
        on_device, mesh=mesh, in_specs=in_specs, out_specs=out_specs, check_vma=False
    )
```

```python
import jax
import jax.numpy as jnp
from jax import lax
from jax.experimental import pallas as pl
from jax.experimental.pallas import tpu as pltpu
from jax.sharding import PartitionSpec as P

LX = 32
LY = 16
MESH = pl.DeviceIdType.MESH
F32 = jnp.float32
BF16 = jnp.bfloat16


def dot(a, b, dims=((1,), (0,))):
    return lax.dot_general(a, b, (dims, ((), ())), preferred_element_type=F32)


def iota(shape, axis):
    return lax.broadcasted_iota(jnp.int32, shape, axis)


def one_hot(hit):
    return jnp.where(hit, 1.0, 0.0).astype(BF16)


def zlo_last(r):
    y, xc, zlo, local = r // 128, (r // 16) % 8, (r // 4) % 4, r % 4
    return y * 128 + zlo * 32 + xc * 4 + local


def zlo_second(r):
    y, zlo, xc, local = r // 128, (r // 32) % 4, (r // 4) % 8, r % 4
    return y * 128 + xc * 16 + zlo * 4 + local


def shift_rows(x, kx, ky, sign):
    n = x.shape[-1]
    x = x.reshape(LX, LY, n)
    for bit in range(4):
        rolled = pltpu.roll(x, (-sign * (1 << bit)) % LY, 1)
        x = jnp.where((ky & (1 << bit)) != 0, rolled, x)
    for bit in range(5):
        s = (sign * (1 << bit)) % LX
        rolled = jnp.concatenate([x[s:], x[:s]], axis=0)
        x = jnp.where((kx & (1 << bit)) != 0, rolled, x)
    return x.reshape(LX * LY, n)


def body(v_hbm, bub_hbm, ord_hbm, mix_hbm, out_hbm,
         v_ref, bub_ref, ord_ref, mix_ref, out_ref,
         tt, ta, tb, tq, pr, pt, da, qq, vb, lad, red,
         xa, r1a, ma, r2a, xs, r3, xb, r0, mid, x1, r1b, mb, r2b, dd,
         in_s, out_s, s1a_s, s1a_r, s2a_s, s2a_r, s3_s, s3_r, s0_s, s0_r, s1b_s, s1b_r, s2b_s, s2b_r):
    f = lax.axis_index("freq")
    m = lax.axis_index("mom")
    core, x, zlo, y = m % 2, (m // 2) % 4, (m // 8) % 4, m // 32
    z = f * 4 + zlo
    here = (y * 4 + x) * 2 + core
    zlo_mix = (zlo + 2) % 4
    slot2 = f * 4 + zlo_mix

    def at_z(freq, low):
        return {"freq": freq, "mom": m - zlo * 8 + low * 8}

    def at_xy(place):
        return {"freq": f, "mom": ((place // 8) * 4 + zlo) * 8 + place % 8}

    loads = [pltpu.make_async_copy(v_hbm.at[q], v_ref.at[q], in_s.at[q]) for q in range(4)]
    loads += [
        pltpu.make_async_copy(a, b, in_s.at[4 + i])
        for i, (a, b) in enumerate(((bub_hbm, bub_ref), (ord_hbm, ord_ref), (mix_hbm, mix_ref)))
    ]
    for i in (0, 4, 5, 1, 2, 3, 6):
        loads[i].start()

    barrier = pltpu.get_barrier_semaphore()

    def greet_z(i, _):
        t = (z + i) % 16
        pl.semaphore_signal(barrier, inc=1, device_id=at_z(t // 4, t % 4), device_id_type=MESH)
        return _

    def greet_xy(i, _):
        pl.semaphore_signal(barrier, inc=1, device_id=at_xy((here + i) % 32), device_id_type=MESH)
        return _

    lax.fori_loop(1, 16, greet_z, 0)
    lax.fori_loop(1, 32, greet_xy, 0)

    def got(ref, sem):
        pltpu.make_async_copy(ref, ref, sem).wait()

    def send1(src, dst, ssem, rsem):
        for j in range(4):
            pltpu.make_async_remote_copy(
                src.at[j], dst.at[f], ssem, rsem,
                device_id=at_z(j, zlo_mix), device_id_type=MESH).start()

    def spread(src, dst, ssem, rsem):
        pltpu.make_async_copy(src.at[here], dst.at[here], rsem).start()

        def one(i, _):
            to = (here + i) % 32
            pltpu.make_async_remote_copy(
                src.at[to], dst.at[here], ssem, rsem, device_id=at_xy(to), device_id_type=MESH).start()
            return _

        lax.fori_loop(1, 32, one, 0)

    def send2(src, dst, ssem, rsem):
        pltpu.make_async_copy(src.at[f, zlo], dst.at[slot2], rsem).start()

        def one(i, _):
            near = (i + 1) // 2
            t = (z + 8 + near - 2 * near * (i % 2)) % 16
            pltpu.make_async_remote_copy(
                src.at[t // 4, t % 4], dst.at[slot2], ssem, rsem,
                device_id=at_z(t // 4, t % 4), device_id_type=MESH).start()
            return _

        lax.fori_loop(0, 15, one, 0)

    def ladder(ql):
        bub = bub_ref[pl.ds(ql, 1), :]
        vb[...] = (v_ref[ql].astype(F32) * bub).astype(BF16)
        for h in range(2):
            rows = pl.ds(h * 256, 256)
            lad[rows, :] = (v_ref[ql, rows, :].astype(F32) + dot(vb[rows, :], v_ref[ql])).astype(BF16)
        red[ql] = dot(vb[:256, :], lad[...]).astype(BF16)

    def coords(h):
        order = ord_ref[:, h * 128:(h + 1) * 128]
        return order // LY, order % LY

    def to_transfer(ql, h, rows):
        point = dot(tt[...], red[ql, h * 128:(h + 1) * 128, :], ((1,), (1,)))
        return dot(rows[...], shift_rows(point, *coords(h), 1).astype(BF16)).astype(BF16)

    def first_a(ql):
        xa[ql] = to_transfer(ql, 0, ta).reshape(4, 128, 128)

    for i in (0, 4, 5):
        loads[i].wait()
    ladder(0)
    order = ord_ref[...]
    tt[...] = one_hot(iota((512, 512), 0) == order)
    for b in range(4):
        column = jnp.transpose(jnp.broadcast_to(order[:, b * 128:(b + 1) * 128], (128, 128)))
        for c in range(4):
            ta[b * 128:(b + 1) * 128, c * 128:(c + 1) * 128] = one_hot(
                column == iota((128, 128), 1) + c * 128)
    first_a(0)
    pl.semaphore_wait(barrier, 46)
    send1(xa.at[0], r1a.at[0], s1a_s.at[0], s1a_r.at[0])
    for i in (1, 2, 3, 6):
        loads[i].wait()

    def more_a(ql, _):
        ladder(ql)
        first_a(ql)
        send1(xa.at[ql], r1a.at[ql], s1a_s.at[ql], s1a_r.at[ql])
        return _

    lax.fori_loop(1, 4, more_a, 0)

    pr[...] = one_hot(zlo_last(iota((512, 1), 0)) == iota((1, 512), 1))
    tb[...] = dot(pr[...], ta[...]).astype(BF16)

    def first_b(ql, _):
        xb[:, pl.ds(ql, 1)] = to_transfer(ql, 1, tb).reshape(32, 1, 16, 128)
        return _

    lax.fori_loop(0, 4, first_b, 0)
    spread(xb, r0, s0_s, s0_r)

    row, col = iota((512, 1), 0), iota((1, 512), 1)
    pt[...] = one_hot(zlo_second(row) == col)
    da[...] = one_hot(zlo_second((row % 128) * 4 + row // 128) == col)
    tq[...] = dot(tt[...], one_hot((row % 128) * 4 + row // 128 == col), ((1,), (1,))).astype(BF16)
    r64 = iota((256, 1), 0)
    qq[...] = one_hot(
        (r64 // 64) * 64 + (r64 % 4) * 16 + ((r64 // 4) % 4) * 4 + (r64 // 16) % 4 == iota((1, 256), 1))

    def mix(src, dst, rsem):
        got(src, rsem)
        parts = [src[b].astype(F32) for b in range(4)]
        for a in range(4):
            total = mix_ref[a, 0] * parts[0]
            for b in range(1, 4):
                total = total + mix_ref[a, b] * parts[b]
            dst[a] = total.astype(BF16).reshape(4, 32, 128)

    def mix_a(ql, _):
        mix(r1a.at[ql], ma.at[ql], s1a_r.at[ql])
        send2(ma.at[ql], r2a.at[ql], s2a_s.at[ql], s2a_r.at[ql])
        return _

    def mix_b(local, _):
        mix(r1b.at[local], mb.at[local], s1b_r.at[local])
        send2(mb.at[local], r2b.at[local], s2b_s.at[local], s2b_r.at[local])
        return _

    lax.fori_loop(0, 2, mix_a, 0)
    got(r0, s0_r)
    for i in range(8):
        rows = r0[i * 4:(i + 1) * 4].reshape(256, 128)
        rows = dot(qq[...], rows).astype(BF16).reshape(4, 4, 16, 128)
        for local in range(4):
            mid[local, i * 4:(i + 1) * 4] = rows[:, local]

    def second_b(local, _):
        x1[local] = dot(pt[...], mid[local].reshape(512, 128)).astype(BF16).reshape(4, 128, 128)
        send1(x1.at[local], r1b.at[local], s1b_s.at[local], s1b_r.at[local])
        return _

    lax.fori_loop(0, 4, second_b, 0)
    lax.fori_loop(2, 4, mix_a, 0)

    def third_a(ql, _):
        got(r2a.at[ql], s2a_r.at[ql])
        xs[ql] = dot(pr[...], r2a[ql].reshape(512, 128)).astype(BF16).reshape(32, 16, 128)
        spread(xs.at[ql], r3.at[ql], s3_s.at[ql], s3_r.at[ql])
        return mix_b(ql, _)

    lax.fori_loop(0, 4, third_a, 0)

    def finish(h, local, table, rows):
        point = dot(table[...], rows.reshape(512, 128))
        moved = jnp.transpose(shift_rows(point, *coords(h), -1)).astype(BF16)
        lines = pl.ds(h * 128, 128)
        out_ref[local, lines, :] = dot(moved, tt[...]).astype(BF16)
        pltpu.make_async_copy(out_ref.at[local, lines], out_hbm.at[local, lines], out_s).start()

    def last_a(ql, _):
        got(r3.at[ql], s3_r.at[ql])
        rows = dot(da[...], r3[ql].reshape(512, 128)).astype(BF16)
        dd[:, pl.ds(ql, 1)] = rows.reshape(4, 1, 128, 128)
        return _

    def finish_a(local, _):
        finish(0, local, tq, dd[local])
        return _

    def finish_b(local, _):
        got(r2b.at[local], s2b_r.at[local])
        finish(1, local, tt, r2b[local])
        return _

    lax.fori_loop(0, 4, last_a, 0)
    lax.fori_loop(0, 4, finish_a, 0)
    lax.fori_loop(0, 4, finish_b, 0)

    def drain(i, _):
        got(xa.at[i], s1a_s.at[i])
        got(x1.at[i], s1b_s.at[i])
        for s in (s2a_s, s2b_s):
            got(ma.at[i, pl.ds(0, 3)], s.at[i])
            got(ma.at[i, 0, pl.ds(0, 3)], s.at[i])
        got(xs.at[i, pl.ds(0, 31)], s3_s.at[i])
        return _

    lax.fori_loop(0, 4, drain, 0)
    got(xb.at[pl.ds(0, 31)], s0_s)
    got(out_ref, out_s)


def on_device(vertex, bubble, mixing, lattice_order):
    def vm(*shape):
        return pltpu.VMEM(shape, BF16)

    sem = pltpu.SemaphoreType.DMA
    out = pl.pallas_call(
        body,
        out_shape=jax.ShapeDtypeStruct((4, 256, 512), BF16),
        in_specs=[pl.BlockSpec(memory_space=pl.ANY)] * 4,
        out_specs=pl.BlockSpec(memory_space=pl.ANY),
        scratch_shapes=[
            vm(4, 512, 512), pltpu.VMEM((4, 512), F32), pltpu.VMEM((1, 512), jnp.int32),
            pltpu.SMEM((4, 4), F32), vm(4, 256, 512),
            vm(512, 512), vm(512, 512), vm(512, 512), vm(512, 512),
            vm(512, 512), vm(512, 512), vm(512, 512), vm(256, 256),
            vm(512, 512), vm(512, 512), vm(4, 256, 512),
            vm(4, 4, 128, 128), vm(4, 4, 128, 128), vm(4, 4, 4, 32, 128), vm(4, 16, 32, 128),
            vm(4, 32, 16, 128), vm(4, 32, 16, 128),
            vm(32, 4, 16, 128), vm(32, 4, 16, 128), vm(4, 32, 16, 128),
            vm(4, 4, 128, 128), vm(4, 4, 128, 128), vm(4, 4, 4, 32, 128), vm(4, 16, 32, 128),
            vm(4, 4, 128, 128),
            sem((7,)), sem, sem((4,)), sem((4,)), sem((4,)), sem((4,)), sem((4,)), sem((4,)),
            sem, sem, sem((4,)), sem((4,)), sem((4,)), sem((4,)),
        ],
        compiler_params=pltpu.CompilerParams(
            collective_id=1, has_side_effects=True, vmem_limit_bytes=56 * 2**20),
        cost_estimate=pl.CostEstimate(flops=4 * 10**9, bytes_accessed=4 * 2**20, transcendentals=0),
    )(vertex[0], bubble[0], lattice_order.reshape(1, 512), mixing)
    return out[None]


def solution(mesh):
    in_specs = (P("freq", "mom", None, None), P("freq", "mom", None), P(), P())
    out_specs = P("freq", "mom", None, None)
    return jax.shard_map(
        on_device, mesh=mesh, in_specs=in_specs, out_specs=out_specs, check_vma=False
    )
```

```python
import jax
import jax.numpy as jnp
from jax import lax
from jax.experimental import pallas as pl
from jax.experimental.pallas import tpu as pltpu
from jax.sharding import PartitionSpec as P

LX = 32
LY = 16
MESH = pl.DeviceIdType.MESH
F32 = jnp.float32
BF16 = jnp.bfloat16


def dot(a, b, dims=((1,), (0,))):
    return lax.dot_general(a, b, (dims, ((), ())), preferred_element_type=F32)


def iota(shape, axis):
    return lax.broadcasted_iota(jnp.int32, shape, axis)


def one_hot(hit):
    return jnp.where(hit, 1.0, 0.0).astype(BF16)


def zlo_last(r):
    y, xc, zlo, local = r // 128, (r // 16) % 8, (r // 4) % 4, r % 4
    return y * 128 + zlo * 32 + xc * 4 + local


def zlo_second(r):
    y, zlo, xc, local = r // 128, (r // 32) % 4, (r // 4) % 8, r % 4
    return y * 128 + xc * 16 + zlo * 4 + local


def shift_rows(x, kx, ky, sign):
    n = x.shape[-1]
    x = x.reshape(LX, LY, n)
    for bit in range(4):
        rolled = pltpu.roll(x, (-sign * (1 << bit)) % LY, 1)
        x = jnp.where((ky & (1 << bit)) != 0, rolled, x)
    for bit in range(5):
        s = (sign * (1 << bit)) % LX
        rolled = jnp.concatenate([x[s:], x[:s]], axis=0)
        x = jnp.where((kx & (1 << bit)) != 0, rolled, x)
    return x.reshape(LX * LY, n)


def body(v_hbm, bub_hbm, ord_hbm, mix_hbm, out_ref,
         v_ref, bub_ref, ord_ref, mix_ref,
         tt, ta, tb, tq, pr, pt, da, qq, vb, lad, red,
         xa, r1a, ma, r2a, xs, r3, xb, r0, mid, x1, r1b, mb, r2b, dd,
         in_s, out_s, s1a_s, s1a_r, s2a_s, s2a_r, s3_s, s3_r, s0_s, s0_r, s1b_s, s1b_r, s2b_s, s2b_r):
    f = lax.axis_index("freq")
    m = lax.axis_index("mom")
    core, x, zlo, y = m % 2, (m // 2) % 4, (m // 8) % 4, m // 32
    z = f * 4 + zlo
    here = (y * 4 + x) * 2 + core
    zlo_mix = (zlo + 2) % 4
    slot2 = f * 4 + zlo_mix

    def at_z(freq, low):
        return {"freq": freq, "mom": m - zlo * 8 + low * 8}

    def at_xy(place):
        return {"freq": f, "mom": ((place // 8) * 4 + zlo) * 8 + place % 8}

    loads = [pltpu.make_async_copy(v_hbm.at[q], v_ref.at[q], in_s.at[q]) for q in range(4)]
    loads += [
        pltpu.make_async_copy(a, b, in_s.at[4 + i])
        for i, (a, b) in enumerate(((bub_hbm, bub_ref), (ord_hbm, ord_ref), (mix_hbm, mix_ref)))
    ]
    for i in (0, 4, 5, 1, 2, 3, 6):
        loads[i].start()

    barrier = pltpu.get_barrier_semaphore()

    def greet_z(i, _):
        t = (z + i) % 16
        pl.semaphore_signal(barrier, inc=1, device_id=at_z(t // 4, t % 4), device_id_type=MESH)
        return _

    def greet_xy(i, _):
        pl.semaphore_signal(barrier, inc=1, device_id=at_xy((here + i) % 32), device_id_type=MESH)
        return _

    lax.fori_loop(1, 16, greet_z, 0)
    lax.fori_loop(1, 32, greet_xy, 0)

    def got(ref, sem):
        pltpu.make_async_copy(ref, ref, sem).wait()

    def send1(src, dst, ssem, rsem):
        for j in range(4):
            pltpu.make_async_remote_copy(
                src.at[j], dst.at[f], ssem, rsem,
                device_id=at_z(j, zlo_mix), device_id_type=MESH).start()

    def spread(src, dst, ssem, rsem):
        pltpu.make_async_copy(src.at[here], dst.at[here], rsem).start()

        def one(i, _):
            to = (here + i) % 32
            pltpu.make_async_remote_copy(
                src.at[to], dst.at[here], ssem, rsem, device_id=at_xy(to), device_id_type=MESH).start()
            return _

        lax.fori_loop(1, 32, one, 0)

    def send2(src, dst, ssem, rsem):
        pltpu.make_async_copy(src.at[f, zlo], dst.at[slot2], rsem).start()

        def one(i, _):
            near = (i + 1) // 2
            t = (z + 8 + near - 2 * near * (i % 2)) % 16
            pltpu.make_async_remote_copy(
                src.at[t // 4, t % 4], dst.at[slot2], ssem, rsem,
                device_id=at_z(t // 4, t % 4), device_id_type=MESH).start()
            return _

        lax.fori_loop(0, 15, one, 0)

    def send2_some(ql, first):
        def one(i, carry):
            near = (i + 1) // 2
            t = (z + 8 + near - 2 * near * (i % 2)) % 16

            @pl.when(t < 4 if first else t >= 4)
            def _():
                pltpu.make_async_remote_copy(
                    mb.at[ql, t // 4, t % 4], r2b.at[ql, slot2], s2b_s.at[ql], s2b_r.at[ql],
                    device_id=at_z(t // 4, t % 4), device_id_type=MESH).start()

            return carry

        lax.fori_loop(0, 15, one, 0)

    def ladder(ql):
        bub = bub_ref[pl.ds(ql, 1), :]
        vb[...] = (v_ref[ql].astype(F32) * bub).astype(BF16)
        for h in range(2):
            rows = pl.ds(h * 256, 256)
            lad[rows, :] = (v_ref[ql, rows, :].astype(F32) + dot(vb[rows, :], v_ref[ql])).astype(BF16)
        red[ql] = dot(vb[:256, :], lad[...]).astype(BF16)

    def coords(h):
        order = ord_ref[:, h * 128:(h + 1) * 128]
        return order // LY, order % LY

    def to_transfer(ql, h, rows):
        point = dot(tt[...], red[ql, h * 128:(h + 1) * 128, :], ((1,), (1,)))
        return dot(rows[...], shift_rows(point, *coords(h), 1).astype(BF16)).astype(BF16)

    def first_a(ql):
        xa[ql] = to_transfer(ql, 0, ta).reshape(4, 128, 128)

    for i in (0, 4, 5):
        loads[i].wait()
    ladder(0)
    order = ord_ref[...]
    tt[...] = one_hot(iota((512, 512), 0) == order)
    for b in range(4):
        column = jnp.transpose(jnp.broadcast_to(order[:, b * 128:(b + 1) * 128], (128, 128)))
        for c in range(4):
            ta[b * 128:(b + 1) * 128, c * 128:(c + 1) * 128] = one_hot(
                column == iota((128, 128), 1) + c * 128)
    first_a(0)
    pl.semaphore_wait(barrier, 46)
    send1(xa.at[0], r1a.at[0], s1a_s.at[0], s1a_r.at[0])
    for i in (1, 2, 3, 6):
        loads[i].wait()

    def more_a(ql, _):
        ladder(ql)
        first_a(ql)
        send1(xa.at[ql], r1a.at[ql], s1a_s.at[ql], s1a_r.at[ql])
        return _

    lax.fori_loop(1, 4, more_a, 0)

    pr[...] = one_hot(zlo_last(iota((512, 1), 0)) == iota((1, 512), 1))
    tb[...] = dot(pr[...], ta[...]).astype(BF16)

    def first_b(ql, _):
        xb[:, pl.ds(ql, 1)] = to_transfer(ql, 1, tb).reshape(32, 1, 16, 128)
        return _

    lax.fori_loop(0, 4, first_b, 0)
    spread(xb, r0, s0_s, s0_r)

    row, col = iota((512, 1), 0), iota((1, 512), 1)
    pt[...] = one_hot(zlo_second(row) == col)
    da[...] = one_hot(zlo_second((row % 128) * 4 + row // 128) == col)
    tq[...] = dot(tt[...], one_hot((row % 128) * 4 + row // 128 == col), ((1,), (1,))).astype(BF16)
    r64 = iota((256, 1), 0)
    qq[...] = one_hot(
        (r64 // 64) * 64 + (r64 % 4) * 16 + ((r64 // 4) % 4) * 4 + (r64 // 16) % 4 == iota((1, 256), 1))

    def mix(src, dst, rsem):
        got(src, rsem)
        parts = [src[b].astype(F32) for b in range(4)]
        for a in range(4):
            total = mix_ref[a, 0] * parts[0]
            for b in range(1, 4):
                total = total + mix_ref[a, b] * parts[b]
            dst[a] = total.astype(BF16).reshape(4, 32, 128)

    def mix_a(ql, _):
        mix(r1a.at[ql], ma.at[ql], s1a_r.at[ql])
        send2(ma.at[ql], r2a.at[ql], s2a_s.at[ql], s2a_r.at[ql])
        return _

    def mix_b(local, _):
        mix(r1b.at[local], mb.at[local], s1b_r.at[local])
        pltpu.make_async_copy(mb.at[local, f, zlo], r2b.at[local, slot2], s2b_r.at[local]).start()
        send2_some(local, True)

        @pl.when(local > 0)
        def _late():
            send2_some(local - 1, False)

        return _

    lax.fori_loop(0, 2, mix_a, 0)
    got(r0, s0_r)
    for i in range(8):
        rows = r0[i * 4:(i + 1) * 4].reshape(256, 128)
        rows = dot(qq[...], rows).astype(BF16).reshape(4, 4, 16, 128)
        for local in range(4):
            mid[local, i * 4:(i + 1) * 4] = rows[:, local]

    def second_b(local, _):
        x1[local] = dot(pt[...], mid[local].reshape(512, 128)).astype(BF16).reshape(4, 128, 128)
        send1(x1.at[local], r1b.at[local], s1b_s.at[local], s1b_r.at[local])
        return _

    lax.fori_loop(0, 4, second_b, 0)
    lax.fori_loop(2, 4, mix_a, 0)

    def third_a(ql, _):
        got(r2a.at[ql], s2a_r.at[ql])
        xs[ql] = dot(pr[...], r2a[ql].reshape(512, 128)).astype(BF16).reshape(32, 16, 128)
        spread(xs.at[ql], r3.at[ql], s3_s.at[ql], s3_r.at[ql])
        return mix_b(ql, _)

    lax.fori_loop(0, 4, third_a, 0)
    send2_some(3, False)

    def finish(h, local, table, rows):
        point = dot(table[...], rows.reshape(512, 128))
        moved = jnp.transpose(shift_rows(point, *coords(h), -1)).astype(BF16)
        lines = pl.ds(h * 128, 128)
        out_ref[local, lines, :] = dot(moved, tt[...]).astype(BF16)

    def last_a(ql, _):
        got(r3.at[ql], s3_r.at[ql])
        rows = dot(da[...], r3[ql].reshape(512, 128)).astype(BF16)
        dd[:, pl.ds(ql, 1)] = rows.reshape(4, 1, 128, 128)
        return _

    def finish_a(local, _):
        finish(0, local, tq, dd[local])
        return _

    def finish_b(local, _):
        got(r2b.at[local], s2b_r.at[local])
        finish(1, local, tt, r2b[local])
        return _

    lax.fori_loop(0, 4, last_a, 0)
    lax.fori_loop(0, 4, finish_a, 0)
    lax.fori_loop(0, 4, finish_b, 0)

    def drain(i, _):
        got(xa.at[i], s1a_s.at[i])
        got(x1.at[i], s1b_s.at[i])
        for s in (s2a_s, s2b_s):
            got(ma.at[i, pl.ds(0, 3)], s.at[i])
            got(ma.at[i, 0, pl.ds(0, 3)], s.at[i])
        got(xs.at[i, pl.ds(0, 31)], s3_s.at[i])
        return _

    lax.fori_loop(0, 4, drain, 0)
    got(xb.at[pl.ds(0, 31)], s0_s)


def on_device(vertex, bubble, mixing, lattice_order):
    def vm(*shape):
        return pltpu.VMEM(shape, BF16)

    sem = pltpu.SemaphoreType.DMA
    out = pl.pallas_call(
        body,
        out_shape=pltpu.VMEM((4, 256, 512), BF16),
        in_specs=[pl.BlockSpec(memory_space=pl.ANY)] * 4,
        out_specs=pl.BlockSpec(memory_space=pltpu.VMEM),
        scratch_shapes=[
            vm(4, 512, 512), pltpu.VMEM((4, 512), F32), pltpu.VMEM((1, 512), jnp.int32),
            pltpu.SMEM((4, 4), F32),
            vm(512, 512), vm(512, 512), vm(512, 512), vm(512, 512),
            vm(512, 512), vm(512, 512), vm(512, 512), vm(256, 256),
            vm(512, 512), vm(512, 512), vm(4, 256, 512),
            vm(4, 4, 128, 128), vm(4, 4, 128, 128), vm(4, 4, 4, 32, 128), vm(4, 16, 32, 128),
            vm(4, 32, 16, 128), vm(4, 32, 16, 128),
            vm(32, 4, 16, 128), vm(32, 4, 16, 128), vm(4, 32, 16, 128),
            vm(4, 4, 128, 128), vm(4, 4, 128, 128), vm(4, 4, 4, 32, 128), vm(4, 16, 32, 128),
            vm(4, 4, 128, 128),
            sem((7,)), sem, sem((4,)), sem((4,)), sem((4,)), sem((4,)), sem((4,)), sem((4,)),
            sem, sem, sem((4,)), sem((4,)), sem((4,)), sem((4,)),
        ],
        compiler_params=pltpu.CompilerParams(
            collective_id=1, has_side_effects=True, vmem_limit_bytes=56 * 2**20),
        cost_estimate=pl.CostEstimate(flops=4 * 10**9, bytes_accessed=4 * 2**20, transcendentals=0),
    )(vertex[0], bubble[0], lattice_order.reshape(1, 512), mixing)
    return out[None]


def solution(mesh):
    in_specs = (P("freq", "mom", None, None), P("freq", "mom", None), P(), P())
    out_specs = P("freq", "mom", None, None)
    return jax.shard_map(
        on_device, mesh=mesh, in_specs=in_specs, out_specs=out_specs, check_vma=False
    )
```

```python
import jax
import jax.numpy as jnp
from jax import lax
from jax.experimental import pallas as pl
from jax.experimental.pallas import tpu as pltpu
from jax.sharding import PartitionSpec as P

LX = 32
LY = 16
MESH = pl.DeviceIdType.MESH
F32 = jnp.float32
BF16 = jnp.bfloat16


def dot(a, b, dims=((1,), (0,))):
    return lax.dot_general(a, b, (dims, ((), ())), preferred_element_type=F32)


def iota(shape, axis):
    return lax.broadcasted_iota(jnp.int32, shape, axis)


def one_hot(hit):
    return jnp.where(hit, 1.0, 0.0).astype(BF16)


def zlo_last(r):
    y, xc, zlo, local = r // 128, (r // 16) % 8, (r // 4) % 4, r % 4
    return y * 128 + zlo * 32 + xc * 4 + local


def zlo_second(r):
    y, zlo, xc, local = r // 128, (r // 32) % 4, (r // 4) % 8, r % 4
    return y * 128 + xc * 16 + zlo * 4 + local


def shift_rows(x, kx, ky, sign):
    n = x.shape[-1]
    x = x.reshape(LX, LY, n)
    for bit in range(4):
        rolled = pltpu.roll(x, (-sign * (1 << bit)) % LY, 1)
        x = jnp.where((ky & (1 << bit)) != 0, rolled, x)
    for bit in range(5):
        s = (sign * (1 << bit)) % LX
        rolled = jnp.concatenate([x[s:], x[:s]], axis=0)
        x = jnp.where((kx & (1 << bit)) != 0, rolled, x)
    return x.reshape(LX * LY, n)


def body(v_hbm, bub_hbm, ord_hbm, mix_hbm, out_ref,
         v_ref, bub_ref, ord_ref, mix_ref,
         tt, ta, tb, tq, pr, pt, da, qq, vb, lad, red,
         xa, r1a, ma, r2a, xs, r3, xb, r0, mid, x1, r1b, mb, r2b, dd,
         sides_s, rows_s, in_s, s1a_s, s1a_r, s2a_s, s2a_r, s3_s, s3_r, s0_s, s0_r, s1b_s, s1b_r, s2b_s, s2b_r):
    f = lax.axis_index("freq")
    m = lax.axis_index("mom")
    core, x, zlo, y = m % 2, (m // 2) % 4, (m // 8) % 4, m // 32
    z = f * 4 + zlo
    here = (y * 4 + x) * 2 + core
    zlo_mix = (zlo + 2) % 4
    slot2 = f * 4 + zlo_mix

    def at_z(freq, low):
        return {"freq": freq, "mom": m - zlo * 8 + low * 8}

    def at_xy(place):
        return {"freq": f, "mom": ((place // 8) * 4 + zlo) * 8 + place % 8}

    def greet(semaphore, device):
        pl.semaphore_signal(semaphore, inc=1, device_id=device, device_id_type=MESH)

    barrier = pltpu.get_barrier_semaphore()
    row = m % 8
    z_sides = [at_z(((z + d) % 16) // 4, (zlo + d) % 4) for d in (1, 15)]
    other_rows = [{"freq": f, "mom": (m + 32 * d) % 128} for d in range(1, 4)]
    for j in range(4):
        greet(barrier, at_z(j, zlo_mix))
    for device in z_sides + other_rows:
        greet(barrier, device)
    for d in range(1, 8):
        greet(barrier, {"freq": f, "mom": m - row + (row + d) % 8})

    loads = [pltpu.make_async_copy(v_hbm.at[q], v_ref.at[q], in_s.at[q]) for q in range(4)]
    loads += [
        pltpu.make_async_copy(a, b, in_s.at[4 + i])
        for i, (a, b) in enumerate(((bub_hbm, bub_ref), (ord_hbm, ord_ref), (mix_hbm, mix_ref)))
    ]
    for i in (0, 4, 5, 1, 2, 3, 6):
        loads[i].start()

    def got(ref, sem):
        pltpu.make_async_copy(ref, ref, sem).wait()

    def send1(src, dst, ssem, rsem):
        for j in range(4):
            pltpu.make_async_remote_copy(
                src.at[j], dst.at[f], ssem, rsem,
                device_id=at_z(j, zlo_mix), device_id_type=MESH).start()

    def spread(src, dst, ssem, rsem):
        pltpu.make_async_copy(src.at[here], dst.at[here], rsem).start()

        def one(i, _):
            to = (here + i) % 32
            pltpu.make_async_remote_copy(
                src.at[to], dst.at[here], ssem, rsem, device_id=at_xy(to), device_id_type=MESH).start()
            return _

        lax.fori_loop(1, 32, one, 0)

    def send2(src, dst, ssem, rsem):
        pltpu.make_async_copy(src.at[f, zlo], dst.at[slot2], rsem).start()

        def one(i, _):
            near = (i + 1) // 2
            t = (z + 8 + near - 2 * near * (i % 2)) % 16
            pltpu.make_async_remote_copy(
                src.at[t // 4, t % 4], dst.at[slot2], ssem, rsem,
                device_id=at_z(t // 4, t % 4), device_id_type=MESH).start()
            return _

        lax.fori_loop(0, 15, one, 0)

    def send2_some(ql, first):
        def one(i, carry):
            near = (i + 1) // 2
            t = (z + 8 + near - 2 * near * (i % 2)) % 16

            @pl.when(t < 4 if first else t >= 4)
            def _():
                pltpu.make_async_remote_copy(
                    mb.at[ql, t // 4, t % 4], r2b.at[ql, slot2], s2b_s.at[ql], s2b_r.at[ql],
                    device_id=at_z(t // 4, t % 4), device_id_type=MESH).start()

            return carry

        lax.fori_loop(0, 15, one, 0)

    def ladder(ql):
        bub = bub_ref[pl.ds(ql, 1), :]
        vb[...] = (v_ref[ql].astype(F32) * bub).astype(BF16)
        for h in range(2):
            rows = pl.ds(h * 256, 256)
            lad[rows, :] = (v_ref[ql, rows, :].astype(F32) + dot(vb[rows, :], v_ref[ql])).astype(BF16)
        red[ql] = dot(vb[:256, :], lad[...]).astype(BF16)

    def coords(h):
        order = ord_ref[:, h * 128:(h + 1) * 128]
        return order // LY, order % LY

    def to_transfer(ql, h, rows):
        point = dot(tt[...], red[ql, h * 128:(h + 1) * 128, :], ((1,), (1,)))
        return dot(rows[...], shift_rows(point, *coords(h), 1).astype(BF16)).astype(BF16)

    def first_a(ql):
        xa[ql] = to_transfer(ql, 0, ta).reshape(4, 128, 128)

    for i in (0, 4, 5):
        loads[i].wait()
    ladder(0)
    order = ord_ref[...]
    tt[...] = one_hot(iota((512, 512), 0) == order)
    for b in range(4):
        column = jnp.transpose(jnp.broadcast_to(order[:, b * 128:(b + 1) * 128], (128, 128)))
        for c in range(4):
            ta[b * 128:(b + 1) * 128, c * 128:(c + 1) * 128] = one_hot(
                column == iota((128, 128), 1) + c * 128)
    first_a(0)
    pl.semaphore_wait(barrier, 16)
    for device in z_sides:
        greet(sides_s, device)
    for device in other_rows:
        greet(rows_s, device)
    send1(xa.at[0], r1a.at[0], s1a_s.at[0], s1a_r.at[0])
    for i in (1, 2, 3, 6):
        loads[i].wait()

    def more_a(ql, _):
        ladder(ql)
        first_a(ql)
        send1(xa.at[ql], r1a.at[ql], s1a_s.at[ql], s1a_r.at[ql])
        return _

    lax.fori_loop(1, 4, more_a, 0)

    pr[...] = one_hot(zlo_last(iota((512, 1), 0)) == iota((1, 512), 1))
    tb[...] = dot(pr[...], ta[...]).astype(BF16)

    def first_b(ql, _):
        xb[:, pl.ds(ql, 1)] = to_transfer(ql, 1, tb).reshape(32, 1, 16, 128)
        return _

    lax.fori_loop(0, 4, first_b, 0)
    pl.semaphore_wait(rows_s, 3)
    spread(xb, r0, s0_s, s0_r)

    line, col = iota((512, 1), 0), iota((1, 512), 1)
    pt[...] = one_hot(zlo_second(line) == col)
    da[...] = one_hot(zlo_second((line % 128) * 4 + line // 128) == col)
    tq[...] = dot(tt[...], one_hot((line % 128) * 4 + line // 128 == col), ((1,), (1,))).astype(BF16)
    r64 = iota((256, 1), 0)
    qq[...] = one_hot(
        (r64 // 64) * 64 + (r64 % 4) * 16 + ((r64 // 4) % 4) * 4 + (r64 // 16) % 4 == iota((1, 256), 1))

    def mix(src, dst, rsem):
        got(src, rsem)
        parts = [src[b].astype(F32) for b in range(4)]
        for a in range(4):
            total = mix_ref[a, 0] * parts[0]
            for b in range(1, 4):
                total = total + mix_ref[a, b] * parts[b]
            dst[a] = total.astype(BF16).reshape(4, 32, 128)

    def mix_a(ql, _):
        mix(r1a.at[ql], ma.at[ql], s1a_r.at[ql])
        send2(ma.at[ql], r2a.at[ql], s2a_s.at[ql], s2a_r.at[ql])
        return _

    def mix_b(local, _):
        mix(r1b.at[local], mb.at[local], s1b_r.at[local])
        pltpu.make_async_copy(mb.at[local, f, zlo], r2b.at[local, slot2], s2b_r.at[local]).start()
        send2_some(local, True)

        @pl.when(local > 0)
        def _late():
            send2_some(local - 1, False)

        return _

    got(r0, s0_r)
    for i in range(8):
        rows = r0[i * 4:(i + 1) * 4].reshape(256, 128)
        rows = dot(qq[...], rows).astype(BF16).reshape(4, 4, 16, 128)
        for local in range(4):
            mid[local, i * 4:(i + 1) * 4] = rows[:, local]

    def second_b(local, _):
        x1[local] = dot(pt[...], mid[local].reshape(512, 128)).astype(BF16).reshape(4, 128, 128)
        send1(x1.at[local], r1b.at[local], s1b_s.at[local], s1b_r.at[local])
        return _

    lax.fori_loop(0, 4, second_b, 0)
    pl.semaphore_wait(sides_s, 2)
    lax.fori_loop(0, 4, mix_a, 0)

    def third_a(ql, _):
        got(r2a.at[ql], s2a_r.at[ql])
        xs[ql] = dot(pr[...], r2a[ql].reshape(512, 128)).astype(BF16).reshape(32, 16, 128)
        spread(xs.at[ql], r3.at[ql], s3_s.at[ql], s3_r.at[ql])
        return mix_b(ql, _)

    lax.fori_loop(0, 4, third_a, 0)
    send2_some(3, False)

    def finish(h, local, table, rows):
        point = dot(table[...], rows.reshape(512, 128))
        moved = jnp.transpose(shift_rows(point, *coords(h), -1)).astype(BF16)
        lines = pl.ds(h * 128, 128)
        out_ref[local, lines, :] = dot(moved, tt[...]).astype(BF16)

    def last_a(ql, _):
        got(r3.at[ql], s3_r.at[ql])
        rows = dot(da[...], r3[ql].reshape(512, 128)).astype(BF16)
        dd[:, pl.ds(ql, 1)] = rows.reshape(4, 1, 128, 128)
        return _

    def finish_a(local, _):
        finish(0, local, tq, dd[local])
        return _

    def finish_b(local, _):
        got(r2b.at[local], s2b_r.at[local])
        finish(1, local, tt, r2b[local])
        return _

    lax.fori_loop(0, 4, last_a, 0)
    lax.fori_loop(0, 4, finish_a, 0)
    lax.fori_loop(0, 4, finish_b, 0)

    def drain(i, _):
        got(xa.at[i], s1a_s.at[i])
        got(x1.at[i], s1b_s.at[i])
        for s in (s2a_s, s2b_s):
            got(ma.at[i, pl.ds(0, 3)], s.at[i])
            got(ma.at[i, 0, pl.ds(0, 3)], s.at[i])
        got(xs.at[i, pl.ds(0, 31)], s3_s.at[i])
        return _

    lax.fori_loop(0, 4, drain, 0)
    got(xb.at[pl.ds(0, 31)], s0_s)


def on_device(vertex, bubble, mixing, lattice_order):
    def vm(*shape):
        return pltpu.VMEM(shape, BF16)

    sem = pltpu.SemaphoreType.DMA
    out = pl.pallas_call(
        body,
        out_shape=pltpu.VMEM((4, 256, 512), BF16),
        in_specs=[pl.BlockSpec(memory_space=pl.ANY)] * 4,
        out_specs=pl.BlockSpec(memory_space=pltpu.VMEM),
        scratch_shapes=[
            vm(4, 512, 512), pltpu.VMEM((4, 512), F32), pltpu.VMEM((1, 512), jnp.int32),
            pltpu.SMEM((4, 4), F32),
            vm(512, 512), vm(512, 512), vm(512, 512), vm(512, 512),
            vm(512, 512), vm(512, 512), vm(512, 512), vm(256, 256),
            vm(512, 512), vm(512, 512), vm(4, 256, 512),
            vm(4, 4, 128, 128), vm(4, 4, 128, 128), vm(4, 4, 4, 32, 128), vm(4, 16, 32, 128),
            vm(4, 32, 16, 128), vm(4, 32, 16, 128),
            vm(32, 4, 16, 128), vm(32, 4, 16, 128), vm(4, 32, 16, 128),
            vm(4, 4, 128, 128), vm(4, 4, 128, 128), vm(4, 4, 4, 32, 128), vm(4, 16, 32, 128),
            vm(4, 4, 128, 128),
            pltpu.SemaphoreType.REGULAR, pltpu.SemaphoreType.REGULAR,
            sem((7,)), sem((4,)), sem((4,)), sem((4,)), sem((4,)), sem((4,)), sem((4,)),
            sem, sem, sem((4,)), sem((4,)), sem((4,)), sem((4,)),
        ],
        compiler_params=pltpu.CompilerParams(
            collective_id=1, has_side_effects=True, vmem_limit_bytes=56 * 2**20),
        cost_estimate=pl.CostEstimate(flops=4 * 10**9, bytes_accessed=4 * 2**20, transcendentals=0),
    )(vertex[0], bubble[0], lattice_order.reshape(1, 512), mixing)
    return out[None]


def solution(mesh):
    in_specs = (P("freq", "mom", None, None), P("freq", "mom", None), P(), P())
    out_specs = P("freq", "mom", None, None)
    return jax.shard_map(
        on_device, mesh=mesh, in_specs=in_specs, out_specs=out_specs, check_vma=False
    )
```

```python
import jax
import jax.numpy as jnp
from jax import lax
from jax.experimental import pallas as pl
from jax.experimental.pallas import tpu as pltpu
from jax.sharding import PartitionSpec as P

LX = 32
LY = 16
MESH = pl.DeviceIdType.MESH
F32 = jnp.float32
BF16 = jnp.bfloat16


def dot(a, b, dims=((1,), (0,))):
    return lax.dot_general(a, b, (dims, ((), ())), preferred_element_type=F32)


def iota(shape, axis):
    return lax.broadcasted_iota(jnp.int32, shape, axis)


def one_hot(hit):
    return jnp.where(hit, 1.0, 0.0).astype(BF16)


def zlo_last(r):
    y, xc, zlo, local = r // 128, (r // 16) % 8, (r // 4) % 4, r % 4
    return y * 128 + zlo * 32 + xc * 4 + local


def zlo_second(r):
    y, zlo, xc, local = r // 128, (r // 32) % 4, (r // 4) % 8, r % 4
    return y * 128 + xc * 16 + zlo * 4 + local


def shift_rows(x, kx, ky, sign):
    n = x.shape[-1]
    x = x.reshape(LX, LY, n)
    for bit in range(4):
        rolled = pltpu.roll(x, (-sign * (1 << bit)) % LY, 1)
        x = jnp.where((ky & (1 << bit)) != 0, rolled, x)
    for bit in range(5):
        s = (sign * (1 << bit)) % LX
        rolled = jnp.concatenate([x[s:], x[:s]], axis=0)
        x = jnp.where((kx & (1 << bit)) != 0, rolled, x)
    return x.reshape(LX * LY, n)


def body(v_hbm, bub_hbm, ord_hbm, mix_hbm, out_ref,
         v_ref, bub_ref, ord_ref, mix_ref,
         tt, ta, tb, tq, pr, pt, da, qq, vb, lad, red,
         xa, r1a, ma, r2a, xs, r3, xb, r0, mid, x1, r1b, mb, r2b, dd,
         sides_s, rows_s, in_s, s1a_s, s1a_r, s2a_s, s2a_r, s3_s, s3_r, s0_s, s0_r, s1b_s, s1b_r, s2b_s, s2b_r):
    f = lax.axis_index("freq")
    m = lax.axis_index("mom")
    core, x, zlo, y = m % 2, (m // 2) % 4, (m // 8) % 4, m // 32
    z = f * 4 + zlo
    here = (y * 4 + x) * 2 + core
    zlo_mix = (zlo + 2) % 4
    slot2 = f * 4 + zlo_mix

    def at_z(freq, low):
        return {"freq": freq, "mom": m - zlo * 8 + low * 8}

    def at_xy(place):
        return {"freq": f, "mom": ((place // 8) * 4 + zlo) * 8 + place % 8}

    def greet(semaphore, device):
        pl.semaphore_signal(semaphore, inc=1, device_id=device, device_id_type=MESH)

    barrier = pltpu.get_barrier_semaphore()
    row = m % 8
    z_sides = [at_z(((z + d) % 16) // 4, (zlo + d) % 4) for d in (1, 15)]
    other_rows = [{"freq": f, "mom": (m + 32 * d) % 128} for d in range(1, 4)]
    for j in range(4):
        greet(barrier, at_z(j, zlo_mix))
    for device in z_sides + other_rows:
        greet(barrier, device)
    for d in range(1, 8):
        greet(barrier, {"freq": f, "mom": m - row + (row + d) % 8})

    loads = [pltpu.make_async_copy(v_hbm.at[q], v_ref.at[q], in_s.at[q]) for q in range(4)]
    loads += [
        pltpu.make_async_copy(a, b, in_s.at[4 + i])
        for i, (a, b) in enumerate(((bub_hbm, bub_ref), (ord_hbm, ord_ref), (mix_hbm, mix_ref)))
    ]
    for i in (0, 4, 5, 1, 2, 3, 6):
        loads[i].start()

    def got(ref, sem):
        pltpu.make_async_copy(ref, ref, sem).wait()

    def send1(src, dst, ssem, rsem):
        for j in range(4):
            pltpu.make_async_remote_copy(
                src.at[j], dst.at[f], ssem, rsem,
                device_id=at_z(j, zlo_mix), device_id_type=MESH).start()

    def spread(src, dst, ssem, rsem):
        pltpu.make_async_copy(src.at[here], dst.at[here], rsem).start()

        def one(i, _):
            to = (here + i) % 32
            pltpu.make_async_remote_copy(
                src.at[to], dst.at[here], ssem, rsem, device_id=at_xy(to), device_id_type=MESH).start()
            return _

        lax.fori_loop(1, 32, one, 0)

    def send2(src, dst, ssem, rsem):
        pltpu.make_async_copy(src.at[f, zlo], dst.at[slot2], rsem).start()

        def one(i, _):
            near = (i + 1) // 2
            t = (z + 8 + near - 2 * near * (i % 2)) % 16
            pltpu.make_async_remote_copy(
                src.at[t // 4, t % 4], dst.at[slot2], ssem, rsem,
                device_id=at_z(t // 4, t % 4), device_id_type=MESH).start()
            return _

        lax.fori_loop(0, 15, one, 0)

    def send2_some(ql, first):
        def one(i, carry):
            near = (i + 1) // 2
            t = (z + 8 + near - 2 * near * (i % 2)) % 16

            @pl.when(t < 4 if first else t >= 4)
            def _():
                pltpu.make_async_remote_copy(
                    mb.at[ql, t // 4, t % 4], r2b.at[ql, slot2], s2b_s.at[ql], s2b_r.at[ql],
                    device_id=at_z(t // 4, t % 4), device_id_type=MESH).start()

            return carry

        lax.fori_loop(0, 15, one, 0)

    def ladder(ql):
        bub = bub_ref[pl.ds(ql, 1), :]
        vb[...] = (v_ref[ql].astype(F32) * bub).astype(BF16)
        for h in range(2):
            rows = pl.ds(h * 256, 256)
            lad[rows, :] = (v_ref[ql, rows, :].astype(F32) + dot(vb[rows, :], v_ref[ql])).astype(BF16)
        red[ql] = dot(vb[:256, :], lad[...]).astype(BF16)

    def coords(h):
        order = ord_ref[:, h * 128:(h + 1) * 128]
        return order // LY, order % LY

    def to_transfer(ql, h, rows):
        point = dot(tt[...], red[ql, h * 128:(h + 1) * 128, :], ((1,), (1,)))
        return dot(rows[...], shift_rows(point, *coords(h), 1).astype(BF16)).astype(BF16)

    def first_a(ql):
        xa[ql] = to_transfer(ql, 0, ta).reshape(4, 128, 128)

    for i in (0, 4, 5):
        loads[i].wait()
    ladder(0)
    order = ord_ref[...]
    tt[...] = one_hot(iota((512, 512), 0) == order)
    for b in range(4):
        column = jnp.transpose(jnp.broadcast_to(order[:, b * 128:(b + 1) * 128], (128, 128)))
        for c in range(4):
            ta[b * 128:(b + 1) * 128, c * 128:(c + 1) * 128] = one_hot(
                column == iota((128, 128), 1) + c * 128)
    first_a(0)
    pl.semaphore_wait(barrier, 16)
    for device in z_sides:
        greet(sides_s, device)
    for device in other_rows:
        greet(rows_s, device)
    send1(xa.at[0], r1a.at[0], s1a_s.at[0], s1a_r.at[0])
    for i in (1, 2, 3, 6):
        loads[i].wait()

    def more_a(ql, _):
        ladder(ql)
        first_a(ql)
        send1(xa.at[ql], r1a.at[ql], s1a_s.at[ql], s1a_r.at[ql])
        return _

    lax.fori_loop(1, 4, more_a, 0)

    pr[...] = one_hot(zlo_last(iota((512, 1), 0)) == iota((1, 512), 1))
    tb[...] = dot(pr[...], ta[...]).astype(BF16)

    def first_b(ql, _):
        xb[:, pl.ds(ql, 1)] = to_transfer(ql, 1, tb).reshape(32, 1, 16, 128)
        return _

    lax.fori_loop(0, 4, first_b, 0)
    pl.semaphore_wait(rows_s, 3)
    spread(xb, r0, s0_s, s0_r)

    line, col = iota((512, 1), 0), iota((1, 512), 1)
    pt[...] = one_hot(zlo_second(line) == col)
    da[...] = one_hot(zlo_second((line % 128) * 4 + line // 128) == col)
    tq[...] = dot(tt[...], one_hot((line % 128) * 4 + line // 128 == col), ((1,), (1,))).astype(BF16)
    r64 = iota((256, 1), 0)
    qq[...] = one_hot(
        (r64 // 64) * 64 + (r64 % 4) * 16 + ((r64 // 4) % 4) * 4 + (r64 // 16) % 4 == iota((1, 256), 1))

    def mix(src, dst, rsem):
        got(src, rsem)
        parts = [src[b].astype(F32) for b in range(4)]
        for a in range(4):
            total = mix_ref[a, 0] * parts[0]
            for b in range(1, 4):
                total = total + mix_ref[a, b] * parts[b]
            dst[a] = total.astype(BF16).reshape(4, 32, 128)

    def mix_a(ql, _):
        mix(r1a.at[ql], ma.at[ql], s1a_r.at[ql])
        send2(ma.at[ql], r2a.at[ql], s2a_s.at[ql], s2a_r.at[ql])
        return _

    def mix_b(local, _):
        mix(r1b.at[local], mb.at[local], s1b_r.at[local])
        pltpu.make_async_copy(mb.at[local, f, zlo], r2b.at[local, slot2], s2b_r.at[local]).start()
        send2_some(local, True)

        @pl.when(local > 0)
        def _late():
            send2_some(local - 1, False)

        return _

    pl.semaphore_wait(sides_s, 2)
    lax.fori_loop(0, 1 * core, mix_a, 0)
    got(r0, s0_r)
    for i in range(8):
        rows = r0[i * 4:(i + 1) * 4].reshape(256, 128)
        rows = dot(qq[...], rows).astype(BF16).reshape(4, 4, 16, 128)
        for local in range(4):
            mid[local, i * 4:(i + 1) * 4] = rows[:, local]

    def second_b(local, _):
        x1[local] = dot(pt[...], mid[local].reshape(512, 128)).astype(BF16).reshape(4, 128, 128)
        send1(x1.at[local], r1b.at[local], s1b_s.at[local], s1b_r.at[local])
        return _

    lax.fori_loop(0, 4, second_b, 0)
    lax.fori_loop(1 * core, 4, mix_a, 0)

    def third_a(ql, _):
        got(r2a.at[ql], s2a_r.at[ql])
        xs[ql] = dot(pr[...], r2a[ql].reshape(512, 128)).astype(BF16).reshape(32, 16, 128)
        spread(xs.at[ql], r3.at[ql], s3_s.at[ql], s3_r.at[ql])
        return mix_b(ql, _)

    lax.fori_loop(0, 4, third_a, 0)
    send2_some(3, False)

    def finish(h, local, table, rows):
        point = dot(table[...], rows.reshape(512, 128))
        moved = jnp.transpose(shift_rows(point, *coords(h), -1)).astype(BF16)
        lines = pl.ds(h * 128, 128)
        out_ref[local, lines, :] = dot(moved, tt[...]).astype(BF16)

    def last_a(ql, _):
        got(r3.at[ql], s3_r.at[ql])
        rows = dot(da[...], r3[ql].reshape(512, 128)).astype(BF16)
        dd[:, pl.ds(ql, 1)] = rows.reshape(4, 1, 128, 128)
        return _

    def finish_a(local, _):
        finish(0, local, tq, dd[local])
        return _

    def finish_b(local, _):
        got(r2b.at[local], s2b_r.at[local])
        finish(1, local, tt, r2b[local])
        return _

    lax.fori_loop(0, 4, last_a, 0)
    lax.fori_loop(0, 4, finish_a, 0)
    lax.fori_loop(0, 4, finish_b, 0)

    def drain(i, _):
        got(xa.at[i], s1a_s.at[i])
        got(x1.at[i], s1b_s.at[i])
        for s in (s2a_s, s2b_s):
            got(ma.at[i, pl.ds(0, 3)], s.at[i])
            got(ma.at[i, 0, pl.ds(0, 3)], s.at[i])
        got(xs.at[i, pl.ds(0, 31)], s3_s.at[i])
        return _

    lax.fori_loop(0, 4, drain, 0)
    got(xb.at[pl.ds(0, 31)], s0_s)


def on_device(vertex, bubble, mixing, lattice_order):
    def vm(*shape):
        return pltpu.VMEM(shape, BF16)

    sem = pltpu.SemaphoreType.DMA
    out = pl.pallas_call(
        body,
        out_shape=pltpu.VMEM((4, 256, 512), BF16),
        in_specs=[pl.BlockSpec(memory_space=pl.ANY)] * 4,
        out_specs=pl.BlockSpec(memory_space=pltpu.VMEM),
        scratch_shapes=[
            vm(4, 512, 512), pltpu.VMEM((4, 512), F32), pltpu.VMEM((1, 512), jnp.int32),
            pltpu.SMEM((4, 4), F32),
            vm(512, 512), vm(512, 512), vm(512, 512), vm(512, 512),
            vm(512, 512), vm(512, 512), vm(512, 512), vm(256, 256),
            vm(512, 512), vm(512, 512), vm(4, 256, 512),
            vm(4, 4, 128, 128), vm(4, 4, 128, 128), vm(4, 4, 4, 32, 128), vm(4, 16, 32, 128),
            vm(4, 32, 16, 128), vm(4, 32, 16, 128),
            vm(32, 4, 16, 128), vm(32, 4, 16, 128), vm(4, 32, 16, 128),
            vm(4, 4, 128, 128), vm(4, 4, 128, 128), vm(4, 4, 4, 32, 128), vm(4, 16, 32, 128),
            vm(4, 4, 128, 128),
            pltpu.SemaphoreType.REGULAR, pltpu.SemaphoreType.REGULAR,
            sem((7,)), sem((4,)), sem((4,)), sem((4,)), sem((4,)), sem((4,)), sem((4,)),
            sem, sem, sem((4,)), sem((4,)), sem((4,)), sem((4,)),
        ],
        compiler_params=pltpu.CompilerParams(
            collective_id=1, has_side_effects=True, vmem_limit_bytes=56 * 2**20),
        cost_estimate=pl.CostEstimate(flops=4 * 10**9, bytes_accessed=4 * 2**20, transcendentals=0),
    )(vertex[0], bubble[0], lattice_order.reshape(1, 512), mixing)
    return out[None]


def solution(mesh):
    in_specs = (P("freq", "mom", None, None), P("freq", "mom", None), P(), P())
    out_specs = P("freq", "mom", None, None)
    return jax.shard_map(
        on_device, mesh=mesh, in_specs=in_specs, out_specs=out_specs, check_vma=False
    )
```

```python
import jax
import jax.numpy as jnp
from jax import lax
from jax.experimental import pallas as pl
from jax.experimental.pallas import tpu as pltpu
from jax.sharding import PartitionSpec as P

LX = 32
LY = 16
MESH = pl.DeviceIdType.MESH
F32 = jnp.float32
BF16 = jnp.bfloat16


def dot(a, b, dims=((1,), (0,))):
    return lax.dot_general(a, b, (dims, ((), ())), preferred_element_type=F32)


def iota(shape, axis):
    return lax.broadcasted_iota(jnp.int32, shape, axis)


def one_hot(hit):
    return jnp.where(hit, 1.0, 0.0).astype(BF16)


def zlo_last(r):
    y, xc, zlo, local = r // 128, (r // 16) % 8, (r // 4) % 4, r % 4
    return y * 128 + zlo * 32 + xc * 4 + local


def zlo_second(r):
    y, zlo, xc, local = r // 128, (r // 32) % 4, (r // 4) % 8, r % 4
    return y * 128 + xc * 16 + zlo * 4 + local


def shift_rows(x, kx, ky, sign):
    n = x.shape[-1]
    x = x.reshape(LX, LY, n)
    for bit in range(4):
        rolled = pltpu.roll(x, (-sign * (1 << bit)) % LY, 1)
        x = jnp.where((ky & (1 << bit)) != 0, rolled, x)
    for bit in range(5):
        s = (sign * (1 << bit)) % LX
        rolled = jnp.concatenate([x[s:], x[:s]], axis=0)
        x = jnp.where((kx & (1 << bit)) != 0, rolled, x)
    return x.reshape(LX * LY, n)


def body(v_hbm, bub_hbm, ord_hbm, mix_hbm, out_ref,
         v_ref, bub_ref, ord_ref, mix_ref,
         tt, ta, tb, tq, pr, pt, da, qq, vb, lad, red,
         xa, r1a, ma, r2a, xs, r3, xb, r0, mid, x1, r1b, mb, r2b, dd,
         sides_s, rows_s, in_s, s1a_s, s1a_r, s2a_s, s2a_r, s3_s, s3_r, s0_s, s0_r, s1b_s, s1b_r, s2b_s, s2b_r):
    f = lax.axis_index("freq")
    m = lax.axis_index("mom")
    core, x, zlo, y = m % 2, (m // 2) % 4, (m // 8) % 4, m // 32
    z = f * 4 + zlo
    here = (y * 4 + x) * 2 + core
    zlo_mix = (zlo + 2) % 4
    slot2 = f * 4 + zlo_mix

    def at_z(freq, low):
        return {"freq": freq, "mom": m - zlo * 8 + low * 8}

    def at_xy(place):
        return {"freq": f, "mom": ((place // 8) * 4 + zlo) * 8 + place % 8}

    def greet(semaphore, device):
        pl.semaphore_signal(semaphore, inc=1, device_id=device, device_id_type=MESH)

    barrier = pltpu.get_barrier_semaphore()
    row = m % 8
    z_sides = [at_z(((z + d) % 16) // 4, (zlo + d) % 4) for d in (1, 15)]
    other_rows = [{"freq": f, "mom": (m + 32 * d) % 128} for d in range(1, 4)]
    for j in range(4):
        greet(barrier, at_z(j, zlo_mix))
    for device in z_sides + other_rows:
        greet(barrier, device)
    for d in range(1, 8):
        greet(barrier, {"freq": f, "mom": m - row + (row + d) % 8})

    loads = [pltpu.make_async_copy(v_hbm.at[q], v_ref.at[q], in_s.at[q]) for q in range(4)]
    loads += [
        pltpu.make_async_copy(a, b, in_s.at[4 + i])
        for i, (a, b) in enumerate(((bub_hbm, bub_ref), (ord_hbm, ord_ref), (mix_hbm, mix_ref)))
    ]
    for i in (0, 4, 5, 1, 2, 3, 6):
        loads[i].start()

    def got(ref, sem):
        pltpu.make_async_copy(ref, ref, sem).wait()

    def send1(src, dst, ssem, rsem):
        for j in range(4):
            pltpu.make_async_remote_copy(
                src.at[j], dst.at[f], ssem, rsem,
                device_id=at_z(j, zlo_mix), device_id_type=MESH).start()

    def spread(src, dst, ssem, rsem):
        pltpu.make_async_copy(src.at[here], dst.at[here], rsem).start()

        def one(i, _):
            to = (here + i) % 32
            pltpu.make_async_remote_copy(
                src.at[to], dst.at[here], ssem, rsem, device_id=at_xy(to), device_id_type=MESH).start()
            return _

        lax.fori_loop(1, 32, one, 0)

    def send2(src, dst, ssem, rsem):
        pltpu.make_async_copy(src.at[f, zlo], dst.at[slot2], rsem).start()

        def one(i, _):
            near = (i + 1) // 2
            t = (z + 8 + near - 2 * near * (i % 2)) % 16
            pltpu.make_async_remote_copy(
                src.at[t // 4, t % 4], dst.at[slot2], ssem, rsem,
                device_id=at_z(t // 4, t % 4), device_id_type=MESH).start()
            return _

        lax.fori_loop(0, 15, one, 0)

    def send2_some(ql, first):
        def one(i, carry):
            near = (i + 1) // 2
            t = (z + 8 + near - 2 * near * (i % 2)) % 16

            @pl.when(t < 4 if first else t >= 4)
            def _():
                pltpu.make_async_remote_copy(
                    mb.at[ql, t // 4, t % 4], r2b.at[ql, slot2], s2b_s.at[ql], s2b_r.at[ql],
                    device_id=at_z(t // 4, t % 4), device_id_type=MESH).start()

            return carry

        lax.fori_loop(0, 15, one, 0)

    def ladder(ql):
        bub = bub_ref[pl.ds(ql, 1), :]
        vb[...] = (v_ref[ql].astype(F32) * bub).astype(BF16)
        for h in range(2):
            rows = pl.ds(h * 256, 256)
            lad[rows, :] = (v_ref[ql, rows, :].astype(F32) + dot(vb[rows, :], v_ref[ql])).astype(BF16)
        red[ql] = dot(vb[:256, :], lad[...]).astype(BF16)

    def coords(h):
        order = ord_ref[:, h * 128:(h + 1) * 128]
        return order // LY, order % LY

    def to_transfer(ql, h, rows):
        point = dot(tt[...], red[ql, h * 128:(h + 1) * 128, :], ((1,), (1,)))
        return dot(rows[...], shift_rows(point, *coords(h), 1).astype(BF16)).astype(BF16)

    def first_a(ql):
        xa[ql] = to_transfer(ql, 0, ta).reshape(4, 128, 128)

    for i in (0, 4, 5):
        loads[i].wait()
    ladder(0)
    order = ord_ref[...]
    tt[...] = one_hot(iota((512, 512), 0) == order)
    for b in range(4):
        column = jnp.transpose(jnp.broadcast_to(order[:, b * 128:(b + 1) * 128], (128, 128)))
        for c in range(4):
            ta[b * 128:(b + 1) * 128, c * 128:(c + 1) * 128] = one_hot(
                column == iota((128, 128), 1) + c * 128)
    first_a(0)
    pl.semaphore_wait(barrier, 16)
    for device in z_sides:
        greet(sides_s, device)
    for device in other_rows:
        greet(rows_s, device)
    send1(xa.at[0], r1a.at[0], s1a_s.at[0], s1a_r.at[0])
    for i in (1, 2, 3, 6):
        loads[i].wait()

    def more_a(ql, _):
        ladder(ql)
        first_a(ql)
        send1(xa.at[ql], r1a.at[ql], s1a_s.at[ql], s1a_r.at[ql])
        return _

    lax.fori_loop(1, 4, more_a, 0)

    pr[...] = one_hot(zlo_last(iota((512, 1), 0)) == iota((1, 512), 1))
    tb[...] = dot(pr[...], ta[...]).astype(BF16)

    def first_b(ql, _):
        xb[:, pl.ds(ql, 1)] = to_transfer(ql, 1, tb).reshape(32, 1, 16, 128)
        return _

    lax.fori_loop(0, 4, first_b, 0)
    pl.semaphore_wait(rows_s, 3)
    spread(xb, r0, s0_s, s0_r)

    line, col = iota((512, 1), 0), iota((1, 512), 1)
    pt[...] = one_hot(zlo_second(line) == col)
    da[...] = one_hot(zlo_second((line % 128) * 4 + line // 128) == col)
    tq[...] = dot(tt[...], one_hot((line % 128) * 4 + line // 128 == col), ((1,), (1,))).astype(BF16)
    r64 = iota((256, 1), 0)
    qq[...] = one_hot(
        (r64 // 64) * 64 + (r64 % 4) * 16 + ((r64 // 4) % 4) * 4 + (r64 // 16) % 4 == iota((1, 256), 1))

    def mix(src, dst, rsem):
        got(src, rsem)
        parts = [src[b].astype(F32) for b in range(4)]
        for a in range(4):
            total = mix_ref[a, 0] * parts[0]
            for b in range(1, 4):
                total = total + mix_ref[a, b] * parts[b]
            dst[a] = total.astype(BF16).reshape(4, 32, 128)

    def mix_a(ql, _):
        mix(r1a.at[ql], ma.at[ql], s1a_r.at[ql])
        send2(ma.at[ql], r2a.at[ql], s2a_s.at[ql], s2a_r.at[ql])
        return _

    def mix_b(local, _):
        mix(r1b.at[local], mb.at[local], s1b_r.at[local])
        pltpu.make_async_copy(mb.at[local, f, zlo], r2b.at[local, slot2], s2b_r.at[local]).start()
        send2_some(local, True)

        @pl.when(local + core > 1)
        def _late():
            send2_some(local + core - 2, False)

        return _

    pl.semaphore_wait(sides_s, 2)
    lax.fori_loop(0, 1 * core, mix_a, 0)
    got(r0, s0_r)
    for i in range(8):
        rows = r0[i * 4:(i + 1) * 4].reshape(256, 128)
        rows = dot(qq[...], rows).astype(BF16).reshape(4, 4, 16, 128)
        for local in range(4):
            mid[local, i * 4:(i + 1) * 4] = rows[:, local]

    def second_b(local, _):
        x1[local] = dot(pt[...], mid[local].reshape(512, 128)).astype(BF16).reshape(4, 128, 128)
        send1(x1.at[local], r1b.at[local], s1b_s.at[local], s1b_r.at[local])
        return _

    lax.fori_loop(0, 4, second_b, 0)
    lax.fori_loop(1 * core, 4, mix_a, 0)

    def third_a(ql, _):
        got(r2a.at[ql], s2a_r.at[ql])
        xs[ql] = dot(pr[...], r2a[ql].reshape(512, 128)).astype(BF16).reshape(32, 16, 128)
        spread(xs.at[ql], r3.at[ql], s3_s.at[ql], s3_r.at[ql])
        return mix_b(ql, _)

    lax.fori_loop(0, 4, third_a, 0)

    @pl.when(core == 0)
    def _last():
        send2_some(2, False)

    send2_some(3, False)

    def finish(h, local, table, rows):
        point = dot(table[...], rows.reshape(512, 128))
        moved = jnp.transpose(shift_rows(point, *coords(h), -1)).astype(BF16)
        lines = pl.ds(h * 128, 128)
        out_ref[local, lines, :] = dot(moved, tt[...]).astype(BF16)

    def last_a(ql, _):
        got(r3.at[ql], s3_r.at[ql])
        rows = dot(da[...], r3[ql].reshape(512, 128)).astype(BF16)
        dd[:, pl.ds(ql, 1)] = rows.reshape(4, 1, 128, 128)
        return _

    def finish_a(local, _):
        finish(0, local, tq, dd[local])
        return _

    def finish_b(local, _):
        got(r2b.at[local], s2b_r.at[local])
        finish(1, local, tt, r2b[local])
        return _

    lax.fori_loop(0, 4, last_a, 0)
    lax.fori_loop(0, 4, finish_a, 0)
    lax.fori_loop(0, 4, finish_b, 0)

    def drain(i, _):
        got(xa.at[i], s1a_s.at[i])
        got(x1.at[i], s1b_s.at[i])
        for s in (s2a_s, s2b_s):
            got(ma.at[i, pl.ds(0, 3)], s.at[i])
            got(ma.at[i, 0, pl.ds(0, 3)], s.at[i])
        got(xs.at[i, pl.ds(0, 31)], s3_s.at[i])
        return _

    lax.fori_loop(0, 4, drain, 0)
    got(xb.at[pl.ds(0, 31)], s0_s)


def on_device(vertex, bubble, mixing, lattice_order):
    def vm(*shape):
        return pltpu.VMEM(shape, BF16)

    sem = pltpu.SemaphoreType.DMA
    out = pl.pallas_call(
        body,
        out_shape=pltpu.VMEM((4, 256, 512), BF16),
        in_specs=[pl.BlockSpec(memory_space=pl.ANY)] * 4,
        out_specs=pl.BlockSpec(memory_space=pltpu.VMEM),
        scratch_shapes=[
            vm(4, 512, 512), pltpu.VMEM((4, 512), F32), pltpu.VMEM((1, 512), jnp.int32),
            pltpu.SMEM((4, 4), F32),
            vm(512, 512), vm(512, 512), vm(512, 512), vm(512, 512),
            vm(512, 512), vm(512, 512), vm(512, 512), vm(256, 256),
            vm(512, 512), vm(512, 512), vm(4, 256, 512),
            vm(4, 4, 128, 128), vm(4, 4, 128, 128), vm(4, 4, 4, 32, 128), vm(4, 16, 32, 128),
            vm(4, 32, 16, 128), vm(4, 32, 16, 128),
            vm(32, 4, 16, 128), vm(32, 4, 16, 128), vm(4, 32, 16, 128),
            vm(4, 4, 128, 128), vm(4, 4, 128, 128), vm(4, 4, 4, 32, 128), vm(4, 16, 32, 128),
            vm(4, 4, 128, 128),
            pltpu.SemaphoreType.REGULAR, pltpu.SemaphoreType.REGULAR,
            sem((7,)), sem((4,)), sem((4,)), sem((4,)), sem((4,)), sem((4,)), sem((4,)),
            sem, sem, sem((4,)), sem((4,)), sem((4,)), sem((4,)),
        ],
        compiler_params=pltpu.CompilerParams(
            collective_id=1, has_side_effects=True, vmem_limit_bytes=56 * 2**20),
        cost_estimate=pl.CostEstimate(flops=4 * 10**9, bytes_accessed=4 * 2**20, transcendentals=0),
    )(vertex[0], bubble[0], lattice_order.reshape(1, 512), mixing)
    return out[None]


def solution(mesh):
    in_specs = (P("freq", "mom", None, None), P("freq", "mom", None), P(), P())
    out_specs = P("freq", "mom", None, None)
    return jax.shard_map(
        on_device, mesh=mesh, in_specs=in_specs, out_specs=out_specs, check_vma=False
    )
```
